256 devices in a mesh: comp: 2 (over core), lat: 16 (over z_hi, y), lon: 8 (over x, z_lo).
Axes of the slice: x: 4, y: 4, z: 8 (z_hi: 4, z_lo: 2; z = z_hi * 2 + z_lo), core: 2. Of those that a mesh axis runs over, the one named last changes fastest.
Arguments:
- state: bfloat16 [2, 256, 1024, 384], P('comp', 'lat', 'lon'), may hold values from -6 to 6
- source_cell: int32 [2, 4, 256, 1024], P('comp', None, 'lat', 'lon'), may hold values from 0 to 262143, as said below
- remap_weight: float32 [2, 4, 256, 1024], P('comp', None, 'lat', 'lon'), may hold values from 0.1 to 1
- sea_mask: int32 [2, 256, 1024], P('comp', 'lat', 'lon'), may hold values 0 or 1
- spectral_weight: bfloat16 [2, 384, 384], P('comp'), may hold values from -0.3125 to 0.3125
- cotangent: bfloat16 [2, 256, 1024, 384], P('comp', 'lat', 'lon'), may hold values from -6 to 6
Outputs:
- updated: bfloat16 [2, 256, 1024, 384], P('comp', 'lat', 'lon')
- weight_grad: float32 [2, 384, 384], P('comp')
The draws below stay inside these ranges and needn't reach their ends.
Inputs may be any that keep to these rules, and one draw needn't show every extreme that they name: `source_cell`: A cell index row * 1024 + longitude of the other component's grid; its row differs from the target cell's row by at most 8, and its longitude lies in the same aligned block of 128 longitudes as the target's.
All inputs are finite; a program needn't handle non-finite values. No bound on the sum of `sea_mask` on one device may be relied on, other than what follows from the above.
Results may differ from the reference program's by a relative error of at most 0.0086.
Values may be sent and summed in bfloat16 or wider, within the bound.
No kernel may reach another device: no remote copies, remote signals or barrier semaphores. Data moves between devices by JAX's collectives and lax.ppermute only.
A program may use at most 64 MiB of HBM per device.

```python
import math
import jax
import jax.numpy as jnp

C = 384
NLON = 1024
M = 384
K = 4
NLAT = 256
LON_DEV = 128
REACH = 8


def draw_source_cell(key, part):
    key = jax.random.fold_in(key, 7)
    key_row, key_col = jax.random.split(key)
    shape = (2, K, NLAT, NLON)
    row_ids = jnp.arange(NLAT, dtype=jnp.int32)[None, None, :, None]
    col_ids = jnp.arange(NLON, dtype=jnp.int32)[None, None, None, :]
    offset = jax.random.randint(key_row, shape, -REACH, REACH + 1, dtype=jnp.int32)
    row = jnp.clip(row_ids + offset, 0, NLAT - 1)
    block = col_ids // LON_DEV * LON_DEV
    column = block + jax.random.randint(key_col, shape, 0, LON_DEV, dtype=jnp.int32)
    cells = row * NLON + column
    cells = cells.at[0, 0, 0, 0].set(0)
    cells = cells.at[1, 0, NLAT - 1, NLON - 1].set(NLAT * NLON - 1)
    return cells.astype(jnp.int32)


def touch_ends(result, key, smallest, high):
    shape = result.shape
    index_at = [jax.random.randint(jax.random.fold_in(key, axis), (), 0, shape[axis]) for axis in range(len(shape))]
    result = result.at[tuple(index_at)].set(smallest)
    longest = shape.index(max(shape))
    index_at[longest] = (index_at[longest] + 1) % shape[longest]
    return result.at[tuple(index_at)].set(high)


def shard_levels(key, shape, cuts, smallest, top_value):
    loudness, own = 1.0, jax.random.fold_in(key, 6)
    for position, shards_of in cuts:
        draws = jnp.exp(jax.random.uniform(jax.random.fold_in(own, position), (shards_of,), jnp.float32, smallest / len(cuts), top_value / len(cuts)))
        loudness = loudness * jnp.repeat(draws, shape[position] // shards_of).reshape([-1 if axis == position else 1 for axis in range(len(shape))])
    return loudness


def gaussian(own_key, shape, spread, limit, pieces=(), held_as=jnp.bfloat16):
    entries = jax.random.normal(own_key, shape, jnp.float32) * spread
    if len(pieces) > 0:
        entries = shard_levels(own_key, shape, pieces, -0.22, 0.18) * entries
    return jnp.clip(entries, min=-limit, max=limit).astype(held_as)


def setup_inputs(seed: int = 0) -> dict:
    key_of = jax.random.split(jax.random.key(seed), 7)
    state = gaussian(key_of[0], (2, NLAT, NLON, C), 1.0, 6.0, ((0, 2), (1, 16), (2, 8)))
    source_cell = draw_source_cell(jax.random.fold_in(key_of[6], 71), 0)
    remap_weight = jnp.clip(0.1 + 0.9 * jax.random.uniform(key_of[2], (2, K, NLAT, NLON), jnp.float32) ** shard_levels(key_of[2], (2, K, NLAT, NLON), ((0, 2), (2, 16), (3, 8)), -0.2, 0.2), 0.1, 1.0)
    sea_mask = touch_ends((jax.random.randint(key_of[3], (2, NLAT, NLON), 0, 3) < 2).astype(jnp.int32), jax.random.fold_in(key_of[3], 1), 0, 1)
    spectral_weight = gaussian(key_of[4], (2, C, C), C ** -0.5, 0.3125, ((0, 2),))
    cotangent = gaussian(key_of[5], (2, NLAT, NLON, C), 1.0, 6.0, ((0, 2), (1, 16), (2, 8)))
    return dict(state=state, source_cell=source_cell, remap_weight=remap_weight, sea_mask=sea_mask, spectral_weight=spectral_weight, cotangent=cotangent)


def make_tables(nlon, modes):
    lon_ids = jnp.arange(nlon, dtype=jnp.int32)[:, None]
    mode_ids = jnp.arange(modes, dtype=jnp.int32)[None, :]
    phase = (lon_ids * mode_ids % nlon).astype(jnp.float32)
    angle = phase * jnp.float32(2.0 * math.pi / nlon)
    norm = jnp.float32(1.0 / math.sqrt(nlon))
    table = jnp.concatenate([jnp.cos(angle) * norm, -jnp.sin(angle) * norm], axis=1).astype(jnp.bfloat16)
    factor = jnp.where(mode_ids == 0, 1.0, 2.0).astype(jnp.float32)
    factor = jnp.concatenate([factor, factor], axis=1)
    back_table = (table.astype(jnp.float32) * factor).astype(jnp.bfloat16)
    return (table, back_table)

def one_component(own, other, source_cell, remap_weight, sea_mask, weight, cotangent, table, back_table, scale):
    flat_other = other.reshape(-1, other.shape[-1])
    forcing = jnp.zeros(own.shape, jnp.float32)
    for term in range(K):
        picked = jnp.take(flat_other, source_cell[term], axis=0).astype(jnp.float32)
        forcing = forcing + remap_weight[term][..., None] * picked
    forcing = forcing * sea_mask[..., None].astype(jnp.float32)
    forced = (own.astype(jnp.float32) + forcing).astype(jnp.bfloat16)
    spectra = jnp.einsum('rnc,nk->rkc', forced.astype(jnp.float32), table.astype(jnp.float32)).astype(jnp.bfloat16)
    mixed = jnp.einsum('rkc,cd->rkd', spectra.astype(jnp.float32), weight.astype(jnp.float32)).astype(jnp.bfloat16)
    synth = jnp.einsum('rkd,nk->rnd', mixed.astype(jnp.float32), back_table.astype(jnp.float32))
    sigma = jax.nn.sigmoid(synth)
    updated = (forced.astype(jnp.float32) + synth * sigma).astype(jnp.bfloat16)
    grad_synth = (cotangent.astype(jnp.float32) * sigma * (1.0 + synth * (1.0 - sigma))).astype(jnp.bfloat16)
    grad_spectra = jnp.einsum('rnc,nk->rkc', grad_synth.astype(jnp.float32), back_table.astype(jnp.float32)).astype(jnp.bfloat16)
    grad = jnp.einsum('rkc,rkd->cd', spectra.astype(jnp.float32), grad_spectra.astype(jnp.float32)) * scale
    return (updated, grad)

def reference(state, source_cell, remap_weight, sea_mask, spectral_weight, cotangent):
    table, back_table = make_tables(NLON, M)
    scale = 1.0 / math.sqrt(2 * M * NLAT)
    outs = []
    grads = []
    for comp_id in range(2):
        updated, grad = one_component(state[comp_id], state[1 - comp_id], source_cell[comp_id], remap_weight[comp_id], sea_mask[comp_id], spectral_weight[comp_id], cotangent[comp_id], table, back_table, scale)
        outs.append(updated)
        grads.append(grad)
    return (jnp.stack(outs), jnp.stack(grads))
```

```python
import math

import jax
import jax.numpy as jnp
from jax import lax
from jax.sharding import PartitionSpec as P

M = 384
K = 4
REACH = 8


def partner(block, axis, distance):
    count = lax.axis_size(axis)
    route = []
    for low in range(count):
        high = low | 1 << distance
        if high != low and high < count:
            route += [(low, high), (high, low)]
    return lax.ppermute(block, axis, route)


def with_halo(block, sides, width):
    for axis, dim in sides:
        count = lax.axis_size(axis)
        forward = [(i, i + 1) for i in range(count - 1)]
        backward = [(target, source) for source, target in forward]
        low = lax.ppermute(
            lax.slice_in_dim(block, block.shape[dim] - width, None, axis=dim), axis, forward
        )
        high = lax.ppermute(lax.slice_in_dim(block, 0, width, axis=dim), axis, backward)
        block = jnp.concatenate([low, block, high], axis=dim)
    return block


def make_tables(nlon, modes):
    lon_ids = jnp.arange(nlon, dtype=jnp.int32)[:, None]
    mode_ids = jnp.arange(modes, dtype=jnp.int32)[None, :]
    phase = (lon_ids * mode_ids % nlon).astype(jnp.float32)
    angle = phase * jnp.float32(2.0 * math.pi / nlon)
    norm = jnp.float32(1.0 / math.sqrt(nlon))
    table = jnp.concatenate([jnp.cos(angle) * norm, -jnp.sin(angle) * norm], axis=1).astype(
        jnp.bfloat16
    )
    factor = jnp.where(mode_ids == 0, 1.0, 2.0).astype(jnp.float32)
    factor = jnp.concatenate([factor, factor], axis=1)
    back_table = (table.astype(jnp.float32) * factor).astype(jnp.bfloat16)
    return (table, back_table)


def spread(block, axis):
    return lax.all_to_all(block, axis, split_axis=0, concat_axis=0, tiled=True)


def total(grad, axes):
    rows, columns = grad.shape
    for axis in axes:
        count = lax.axis_size(axis)
        pieces = grad.astype(jnp.bfloat16).reshape(count, -1, columns)
        grad = jnp.sum(spread(pieces, axis).astype(jnp.float32), axis=0)
    grad = grad.astype(jnp.bfloat16)
    for axis in reversed(axes):
        count = lax.axis_size(axis)
        copies = jnp.broadcast_to(grad[None], (count, *grad.shape))
        grad = spread(copies, axis).reshape(-1, columns)
    return grad.astype(jnp.float32)


def local(state, source_cell, remap_weight, sea_mask, spectral_weight, cotangent):
    own = state[0]
    lat_dev, lon_dev, channels = own.shape
    lon_count = lax.axis_size("lon")
    nlon = lon_dev * lon_count
    nlat = lat_dev * lax.axis_size("lat")
    partner_block = partner(own, "comp", 0)
    extended = with_halo(partner_block, (("lat", 0),), REACH)
    flat_other = extended.reshape(-1, channels)
    lat_first = lax.axis_index("lat") * lat_dev - REACH
    lon_first = lax.axis_index("lon") * lon_dev
    cells = source_cell[0]
    local_ids = (cells // nlon - lat_first) * lon_dev + (cells % nlon - lon_first)
    forcing = jnp.zeros(own.shape, jnp.float32)
    for term in range(K):
        picked = jnp.take(flat_other, local_ids[term], axis=0).astype(jnp.float32)
        forcing = forcing + remap_weight[0, term][..., None] * picked
    forcing = forcing * sea_mask[0][..., None].astype(jnp.float32)
    forced = (own.astype(jnp.float32) + forcing).astype(jnp.bfloat16)
    forced_rows = lax.all_to_all(forced, "lon", split_axis=0, concat_axis=1, tiled=True)
    table, back_table = make_tables(nlon, M)
    spectra = jnp.einsum(
        "rnc,nk->rkc", forced_rows, table, preferred_element_type=jnp.float32
    ).astype(jnp.bfloat16)
    mixed = jnp.einsum(
        "rkc,cd->rkd", spectra, spectral_weight[0], preferred_element_type=jnp.float32
    ).astype(jnp.bfloat16)
    synth = jnp.einsum("rkd,nk->rnd", mixed, back_table, preferred_element_type=jnp.float32)
    sigma = jax.nn.sigmoid(synth)
    updated_rows = (forced_rows.astype(jnp.float32) + synth * sigma).astype(jnp.bfloat16)
    updated = lax.all_to_all(updated_rows, "lon", split_axis=1, concat_axis=0, tiled=True)
    grad_rows = lax.all_to_all(cotangent[0], "lon", split_axis=0, concat_axis=1, tiled=True)
    grad_synth = (grad_rows.astype(jnp.float32) * sigma * (1.0 + synth * (1.0 - sigma))).astype(
        jnp.bfloat16
    )
    grad_spectra = jnp.einsum(
        "rnc,nk->rkc", grad_synth, back_table, preferred_element_type=jnp.float32
    ).astype(jnp.bfloat16)
    local_grad = jnp.einsum(
        "rkc,rkd->cd", spectra, grad_spectra, preferred_element_type=jnp.float32
    )
    total_grad = total(local_grad, ("lat", "lon"))
    scale = 1.0 / math.sqrt(2 * M * nlat)
    return (updated[None], (total_grad * scale)[None])


def solution(mesh):
    in_specs = (
        P("comp", "lat", "lon", None),
        P("comp", None, "lat", "lon"),
        P("comp", None, "lat", "lon"),
        P("comp", "lat", "lon"),
        P("comp", None, None),
        P("comp", "lat", "lon", None),
    )
    out_specs = (P("comp", "lat", "lon", None), P("comp", None, None))
    return jax.shard_map(local, mesh=mesh, in_specs=in_specs, out_specs=out_specs, check_vma=False)
```

```python
import math

import jax
import jax.numpy as jnp
import ml_dtypes
import numpy as np
from jax import lax
from jax.experimental import pallas as pl
from jax.experimental.pallas import tpu as pltpu
from jax.sharding import PartitionSpec as P

M = 384
K = 4
REACH = 8
TILE = 128
GROUP = 16
MIB = 1 << 20


def low_pass(nlon, modes):
    phase = (np.arange(nlon)[:, None] * np.arange(modes)[None, :]) % nlon
    angle = phase * (2.0 * math.pi / nlon)
    norm = 1.0 / math.sqrt(nlon)
    table = np.concatenate([np.cos(angle) * norm, -np.sin(angle) * norm], axis=1)
    table = table.astype(np.float32).astype(ml_dtypes.bfloat16).astype(np.float64)
    factor = np.where(np.arange(modes) == 0, 1.0, 2.0)
    factor = np.concatenate([factor, factor])
    return ((table * factor) @ table.T).astype(np.float32).astype(ml_dtypes.bfloat16)


def select_tile(cols, lane):
    tile = jnp.zeros((GROUP, TILE), jnp.float32)
    for term in range(K):
        hit = cols[:, term : term + 1] == lane
        tile = jnp.where(hit, cols[:, K + term : K + term + 1], tile)
    return tile.astype(jnp.bfloat16)


def near_kernel(cols_ref, source_ref, own_ref, partial_ref, edge_ref, near_ref):
    targets, cells = near_ref.shape
    rows = cells // TILE
    lanes = lax.broadcasted_iota(jnp.int32, (GROUP, TILE), 1).astype(jnp.float32)

    def build(group, _):
        start = pl.multiple_of(group * GROUP, GROUP)
        cols = cols_ref[pl.ds(start, GROUP), :]
        for row in range(rows):
            near_ref[pl.ds(start, GROUP), row * TILE : (row + 1) * TILE] = select_tile(
                cols, lanes + float(row * TILE)
            )
        outer = jnp.where(start < targets // 2, -REACH * TILE, cells).astype(jnp.float32)
        for row in range(REACH):
            edge_ref[pl.ds(start, GROUP), row * TILE : (row + 1) * TILE] = select_tile(
                cols, lanes + (outer + float(row * TILE))
            )
        return 0

    lax.fori_loop(0, targets // GROUP, build, 0)

    def add(block, _):
        span = pl.ds(pl.multiple_of(block * 256, 256), 256)
        partial_ref[span, :] = own_ref[span, :].astype(jnp.float32) + jnp.dot(
            near_ref[span, :], source_ref[...], preferred_element_type=jnp.float32
        )
        return 0

    lax.fori_loop(0, targets // 256, add, 0)


def near_part(cols, source, own):
    targets, channels = own.shape
    return pl.pallas_call(
        near_kernel,
        out_shape=(
            jax.ShapeDtypeStruct((targets, channels), jnp.float32),
            jax.ShapeDtypeStruct((targets, REACH * TILE), jnp.bfloat16),
        ),
        in_specs=[pl.BlockSpec(memory_space=pltpu.VMEM)] * 3,
        out_specs=(pl.BlockSpec(memory_space=pltpu.VMEM),) * 2,
        scratch_shapes=[pltpu.VMEM((targets, source.shape[0]), jnp.bfloat16)],
        compiler_params=pltpu.CompilerParams(vmem_limit_bytes=40 * MIB),
        cost_estimate=pl.CostEstimate(
            flops=2 * targets * source.shape[0] * channels, bytes_accessed=16 * MIB, transcendentals=0
        ),
    )(cols, source, own)


def edge_kernel(edge_ref, partial_ref, low_ref, high_ref, forced_ref):
    first = pl.program_id(0) < pl.num_programs(0) // 2

    @pl.when(first)
    def _():
        forced_ref[...] = (
            partial_ref[...] + jnp.dot(edge_ref[...], low_ref[...], preferred_element_type=jnp.float32)
        ).astype(forced_ref.dtype)

    @pl.when(jnp.logical_not(first))
    def _():
        forced_ref[...] = (
            partial_ref[...] + jnp.dot(edge_ref[...], high_ref[...], preferred_element_type=jnp.float32)
        ).astype(forced_ref.dtype)


def edge_part(edge, partial, low, high):
    targets, channels = partial.shape
    block = 512
    return pl.pallas_call(
        edge_kernel,
        grid=(targets // block,),
        out_shape=jax.ShapeDtypeStruct((targets, channels), jnp.bfloat16),
        in_specs=[
            pl.BlockSpec((block, edge.shape[1]), lambda i: (i, 0)),
            pl.BlockSpec((block, channels), lambda i: (i, 0)),
            pl.BlockSpec(low.shape, lambda i: (0, 0)),
            pl.BlockSpec(high.shape, lambda i: (0, 0)),
        ],
        out_specs=pl.BlockSpec((block, channels), lambda i: (i, 0)),
        compiler_params=pltpu.CompilerParams(vmem_limit_bytes=24 * MIB),
        cost_estimate=pl.CostEstimate(
            flops=2 * targets * edge.shape[1] * channels, bytes_accessed=12 * MIB, transcendentals=0
        ),
    )(edge, partial, low, high)


def spectral_kernel(scale, filter_ref, x_ref, cot_ref, weight_ref, out_ref, grad_ref, total_ref):
    row, chunk = pl.program_id(0), pl.program_id(1)
    blocks, _, lon_dev, channels = out_ref.shape
    span = blocks * lon_dev
    x = x_ref[...].reshape(-1, channels)
    smooth = jnp.dot(filter_ref[...], x, preferred_element_type=jnp.float32).astype(jnp.bfloat16)
    synth = jnp.dot(smooth, weight_ref[...], preferred_element_type=jnp.float32)
    sigma = 0.5 + 0.5 * jnp.tanh(0.5 * synth)
    mine = x_ref[pl.ds(chunk * blocks, blocks)].reshape(span, channels).astype(jnp.float32)
    out_ref[...] = (mine + synth * sigma).astype(out_ref.dtype).reshape(out_ref.shape)
    cot = cot_ref[...].reshape(span, channels).astype(jnp.float32)
    grad = (cot * sigma * (1.0 + synth * (1.0 - sigma))).astype(jnp.bfloat16)
    product = lax.dot_general(
        smooth, grad, (((0,), (0,)), ((), ())), preferred_element_type=jnp.float32
    )

    @pl.when(jnp.logical_and(row == 0, chunk == 0))
    def _():
        total_ref[...] = product

    @pl.when(jnp.logical_or(row > 0, chunk > 0))
    def _():
        total_ref[...] += product

    grad_ref[...] = (total_ref[...] * scale).astype(grad_ref.dtype)


def spectral_part(table, x, cot, weight, scale):
    lon_count, rows, lon_dev, channels = x.shape
    nlon = lon_count * lon_dev
    blocks = 2
    chunk = blocks * lon_dev
    return pl.pallas_call(
        lambda *refs: spectral_kernel(scale, *refs),
        grid=(rows, lon_count // blocks),
        out_shape=(
            jax.ShapeDtypeStruct(x.shape, jnp.bfloat16),
            jax.ShapeDtypeStruct((channels, channels), jnp.bfloat16),
        ),
        in_specs=[
            pl.BlockSpec((chunk, nlon), lambda r, c: (c, 0)),
            pl.BlockSpec((lon_count, 1, lon_dev, channels), lambda r, c: (0, r, 0, 0)),
            pl.BlockSpec((blocks, 1, lon_dev, channels), lambda r, c: (c, r, 0, 0)),
            pl.BlockSpec((channels, channels), lambda r, c: (0, 0)),
        ],
        out_specs=(
            pl.BlockSpec((blocks, 1, lon_dev, channels), lambda r, c: (c, r, 0, 0)),
            pl.BlockSpec((channels, channels), lambda r, c: (0, 0)),
        ),
        scratch_shapes=[pltpu.VMEM((channels, channels), jnp.float32)],
        compiler_params=pltpu.CompilerParams(vmem_limit_bytes=24 * MIB),
        cost_estimate=pl.CostEstimate(
            flops=2 * rows * nlon * channels * (nlon + 2 * channels),
            bytes_accessed=8 * MIB,
            transcendentals=rows * nlon * channels,
        ),
    )(table, x, cot, weight)


def spread(block, axis):
    return lax.all_to_all(block, axis, split_axis=0, concat_axis=0, tiled=True)


def ring_sum(piece, axis, step, count):
    size = lax.axis_size(axis)
    total = piece.astype(jnp.float32)
    for shift in range(1, count):
        route = []
        for source in range(size):
            place = source // step % count
            route.append((source, source + ((place + shift) % count - place) * step))
        total = total + lax.ppermute(piece, axis, route).astype(jnp.float32)
    return total.astype(jnp.bfloat16)


def total(grad):
    rows, columns = grad.shape
    count = lax.axis_size("lon")
    pieces = spread(grad.reshape(count, -1, columns), "lon")
    piece = jnp.sum(pieces.astype(jnp.float32), axis=0).astype(jnp.bfloat16)
    piece = ring_sum(piece, "lat", 1, 4)
    piece = ring_sum(piece, "lat", 4, 4)
    copies = jnp.broadcast_to(piece[None], (count, *piece.shape))
    return spread(copies, "lon").reshape(rows, columns).astype(jnp.float32)


def halo_routes(lat_count):
    upward, downward = [], []
    for comp in range(2):
        for low in range(lat_count - 1):
            here = comp * lat_count + low
            there = (1 - comp) * lat_count + low + 1
            upward.append((here, there))
            downward.append((comp * lat_count + low + 1, (1 - comp) * lat_count + low))
    return upward, downward


def local(state, source_cell, remap_weight, sea_mask, spectral_weight, cotangent):
    own = state[0]
    lat_dev, lon_dev, channels = own.shape
    lon_count = lax.axis_size("lon")
    lat_count = lax.axis_size("lat")
    nlon = lon_dev * lon_count
    nlat = lat_dev * lat_count
    targets = lat_dev * lon_dev

    upward, downward = halo_routes(lat_count)
    source = lax.ppermute(own, "comp", [(0, 1), (1, 0)])
    low = lax.ppermute(own[lat_dev - REACH :], ("comp", "lat"), upward)
    high = lax.ppermute(own[:REACH], ("comp", "lat"), downward)
    cot = spread(cotangent[0], "lon").reshape(lon_count, -1, lon_dev, channels)

    cells = source_cell[0]
    lat_first = lax.axis_index("lat") * lat_dev
    place = (cells // nlon - lat_first) * lon_dev + cells % lon_dev
    weight = remap_weight[0] * sea_mask[0][None].astype(jnp.float32)
    merged = [weight[0]]
    for term in range(1, K):
        value = weight[term]
        for other in range(term):
            value = value + jnp.where(place[other] == place[term], weight[other], 0.0)
        merged.append(value)
    cols = jnp.concatenate([place.astype(jnp.float32), jnp.stack(merged)], axis=0)
    cols = cols.reshape(2 * K, targets).T

    flat = lambda block: block.reshape(-1, channels)
    partial, edge = near_part(cols, flat(source), flat(own))
    forced = edge_part(edge, partial, flat(low), flat(high))
    forced = spread(forced.reshape(own.shape), "lon").reshape(cot.shape)
    table = jnp.asarray(low_pass(nlon, M))
    scale = 1.0 / math.sqrt(2 * M * nlat)
    updated, grad = spectral_part(table, forced, cot, spectral_weight[0], scale)
    updated = spread(updated.reshape(own.shape), "lon")
    return (updated[None], total(grad)[None])


def solution(mesh):
    in_specs = (
        P("comp", "lat", "lon", None),
        P("comp", None, "lat", "lon"),
        P("comp", None, "lat", "lon"),
        P("comp", "lat", "lon"),
        P("comp", None, None),
        P("comp", "lat", "lon", None),
    )
    out_specs = (P("comp", "lat", "lon", None), P("comp", None, None))
    return jax.shard_map(local, mesh=mesh, in_specs=in_specs, out_specs=out_specs, check_vma=False)
```

```python
import math

import jax
import jax.numpy as jnp
import ml_dtypes
import numpy as np
from jax import lax
from jax.experimental import pallas as pl
from jax.experimental.pallas import tpu as pltpu
from jax.sharding import PartitionSpec as P

M = 384
K = 4
REACH = 8
QUAD = 4
SPAN = 512
RING = 4
CLOSE = 5
NLON_BITS = 10
MIB = 1 << 20


def low_pass(nlon, modes):
    phase = (np.arange(nlon)[:, None] * np.arange(modes)[None, :]) % nlon
    angle = phase * (2.0 * math.pi / nlon)
    norm = 1.0 / math.sqrt(nlon)
    table = np.concatenate([np.cos(angle) * norm, -np.sin(angle) * norm], axis=1)
    table = table.astype(np.float32).astype(ml_dtypes.bfloat16).astype(np.float64)
    factor = np.where(np.arange(modes) == 0, 1.0, 2.0)
    factor = np.concatenate([factor, factor])
    return ((table * factor) @ table.T).astype(np.float32).astype(ml_dtypes.bfloat16)


def near_kernel(
    lat_ref, cell_ref, weight_ref, mask_ref, source_ref, own_ref,
    partial_ref, close_ref, far_ref, place_ref, merged_ref, near_ref,
):
    rows, lon_dev = mask_ref.shape
    first = lat_ref[0] * rows
    sea = mask_ref[...].astype(jnp.float32)
    for term in range(K):
        cell = cell_ref[term]
        place_ref[term] = (lax.shift_right_logical(cell, NLON_BITS) - first) * lon_dev + (
            cell & (lon_dev - 1)
        )
    for term in range(K):
        value = weight_ref[term]
        for other in range(term):
            value = value + jnp.where(place_ref[other] == place_ref[term], weight_ref[other], 0.0)
        merged_ref[term] = value * sea
    ids = lax.broadcasted_iota(jnp.int16, (lon_dev, lon_dev), 0)

    def lines(row):
        place = [place_ref[t, row : row + 1, :].astype(jnp.int16) for t in range(K)]
        share = [merged_ref[t, row : row + 1, :].astype(jnp.bfloat16) for t in range(K)]
        return place, share

    def tile(place, share, start):
        cells = ids + jnp.asarray(start * lon_dev, jnp.int32).astype(jnp.int16)
        out = jnp.zeros((lon_dev, lon_dev), jnp.bfloat16)
        for term in range(K):
            out = jnp.where(place[term] == cells, share[term], out)
        return out

    half = rows // 2
    for row in range(rows):
        place, share = lines(row)
        span = slice(row * lon_dev, (row + 1) * lon_dev)
        low, high = band(row // QUAD, rows)

        def build(source, _):
            at = pl.multiple_of(source * lon_dev, lon_dev)
            near_ref[pl.ds(at, lon_dev), span] = tile(place, share, source)
            return 0

        lax.fori_loop(low, high, build, 0)
        close_first = -CLOSE if row < half else rows

        def build_close(source, _):
            at = pl.multiple_of(source * lon_dev, lon_dev)
            close_ref[pl.ds(at, lon_dev), span] = tile(place, share, source + close_first)
            return 0

        lax.fori_loop(0, CLOSE, build_close, 0)
        if row < QUAD or row >= rows - QUAD:
            far_first = -REACH if row < half else rows + CLOSE
            place_at = row if row < half else row - rows + 2 * QUAD
            far_span = slice(place_at * lon_dev, (place_at + 1) * lon_dev)
            for source in range(REACH - CLOSE):
                far_ref[source * lon_dev : (source + 1) * lon_dev, far_span] = tile(
                    place, share, source + far_first
                )
    size = QUAD * lon_dev
    for block in range(rows // QUAD):
        low, high = band(block, rows)
        span = slice(block * size, (block + 1) * size)
        partial_ref[span, :] = own_ref[span, :].astype(jnp.float32) + across(
            near_ref[low * lon_dev : high * lon_dev, span],
            source_ref[low * lon_dev : high * lon_dev, :],
        )


def across(left, right):
    return lax.dot_general(
        left, right, (((0,), (0,)), ((), ())), preferred_element_type=jnp.float32
    )


def band(block, rows):
    return max(0, block * QUAD - REACH), min(rows, block * QUAD + QUAD + REACH)


def near_part(lat, cells, weight, mask, source, own):
    targets, channels = own.shape
    rows, lon_dev = mask.shape
    vmem = pl.BlockSpec(memory_space=pltpu.VMEM)
    return pl.pallas_call(
        near_kernel,
        out_shape=(
            jax.ShapeDtypeStruct((targets, channels), jnp.float32),
            jax.ShapeDtypeStruct((CLOSE * lon_dev, targets), jnp.bfloat16),
            jax.ShapeDtypeStruct(((REACH - CLOSE) * lon_dev, 2 * QUAD * lon_dev), jnp.bfloat16),
        ),
        in_specs=[pl.BlockSpec(memory_space=pltpu.SMEM)] + [vmem] * 5,
        out_specs=(vmem,) * 3,
        scratch_shapes=[
            pltpu.VMEM(cells.shape, jnp.int32),
            pltpu.VMEM(cells.shape, jnp.float32),
            pltpu.VMEM((targets, targets), jnp.bfloat16),
        ],
        compiler_params=pltpu.CompilerParams(vmem_limit_bytes=40 * MIB),
        cost_estimate=pl.CostEstimate(
            flops=2 * targets * targets * channels, bytes_accessed=16 * MIB, transcendentals=0
        ),
    )(lat, cells, weight, mask, source, own)


def edge_kernel(close_ref, far_ref, partial_ref, low_close_ref, low_far_ref, high_close_ref, high_far_ref, forced_ref):
    step, last = pl.program_id(0), pl.num_programs(0) - 1

    def put(block_ref, distant_ref):
        value = partial_ref[...] + across(close_ref[...], block_ref[...])
        if distant_ref is not None:
            value = value + across(far_ref[...], distant_ref[...])
        forced_ref[...] = value.astype(forced_ref.dtype)

    pl.when(step == 0)(lambda: put(low_close_ref, low_far_ref))
    pl.when(step == 1)(lambda: put(low_close_ref, None))
    pl.when(step == last - 1)(lambda: put(high_close_ref, None))
    pl.when(step == last)(lambda: put(high_close_ref, high_far_ref))


def edge_part(close, far, partial, low_close, low_far, high_close, high_far):
    targets, channels = partial.shape
    steps = 4
    block = targets // steps
    whole = lambda array: pl.BlockSpec(array.shape, lambda i: (0, 0))
    return pl.pallas_call(
        edge_kernel,
        grid=(steps,),
        out_shape=jax.ShapeDtypeStruct((targets, channels), jnp.bfloat16),
        in_specs=[
            pl.BlockSpec((close.shape[0], block), lambda i: (0, i)),
            pl.BlockSpec((far.shape[0], block), lambda i: (0, i // 2)),
            pl.BlockSpec((block, channels), lambda i: (i, 0)),
            whole(low_close), whole(low_far), whole(high_close), whole(high_far),
        ],
        out_specs=pl.BlockSpec((block, channels), lambda i: (i, 0)),
        compiler_params=pltpu.CompilerParams(vmem_limit_bytes=24 * MIB),
        cost_estimate=pl.CostEstimate(
            flops=2 * targets * close.shape[0] * channels, bytes_accessed=10 * MIB, transcendentals=0
        ),
    )(close, far, partial, low_close, low_far, high_close, high_far)


def spectral_kernel(scale, span, filter_ref, x_ref, cot_ref, weight_ref, out_ref, grad_ref, total_ref):
    row, last = pl.program_id(0), pl.num_programs(0) - 1
    lon_count, _, lon_dev, channels = x_ref.shape
    x = x_ref[...].reshape(-1, channels)
    total = jnp.zeros((channels, channels), jnp.float32)
    for chunk in range(x.shape[0] // span):
        part = slice(chunk * span, (chunk + 1) * span)
        blocks = slice(part.start // lon_dev, part.stop // lon_dev)
        smooth = jnp.dot(filter_ref[part, :], x, preferred_element_type=jnp.float32).astype(jnp.bfloat16)
        synth = jnp.dot(smooth, weight_ref[...], preferred_element_type=jnp.float32)
        sigma = 0.5 + 0.5 * jnp.tanh(0.5 * synth)
        mine = x_ref[blocks].reshape(span, channels).astype(jnp.float32)
        out_ref[blocks] = (mine + synth * sigma).astype(out_ref.dtype).reshape(-1, 1, lon_dev, channels)
        cot = cot_ref[blocks].reshape(span, channels).astype(jnp.float32)
        grad = (cot * sigma * (1.0 + synth * (1.0 - sigma))).astype(jnp.bfloat16)
        total = total + across(smooth, grad)

    @pl.when(row == 0)
    def _():
        total_ref[...] = total

    @pl.when(row > 0)
    def _():
        total_ref[...] += total

    @pl.when(row == last)
    def _():
        grad_ref[...] = (total_ref[...] * scale).astype(grad_ref.dtype)


def spectral_part(table, x, cot, weight, scale, span=SPAN):
    lon_count, rows, lon_dev, channels = x.shape
    nlon = lon_count * lon_dev
    whole = lambda r: (0, 0)
    lines = pl.BlockSpec((lon_count, 1, lon_dev, channels), lambda r: (0, r, 0, 0))
    return pl.pallas_call(
        lambda *refs: spectral_kernel(scale, span, *refs),
        grid=(rows,),
        out_shape=(
            jax.ShapeDtypeStruct(x.shape, jnp.bfloat16),
            jax.ShapeDtypeStruct((channels, channels), jnp.bfloat16),
        ),
        in_specs=[pl.BlockSpec((nlon, nlon), whole), lines, lines, pl.BlockSpec((channels, channels), whole)],
        out_specs=(lines, pl.BlockSpec((channels, channels), whole)),
        scratch_shapes=[pltpu.VMEM((channels, channels), jnp.float32)],
        compiler_params=pltpu.CompilerParams(vmem_limit_bytes=32 * MIB),
        cost_estimate=pl.CostEstimate(
            flops=2 * rows * nlon * channels * (nlon + 2 * channels),
            bytes_accessed=8 * MIB,
            transcendentals=rows * nlon * channels,
        ),
    )(table, x, cot, weight)


def spread(block, axis):
    return lax.all_to_all(block, axis, split_axis=0, concat_axis=0, tiled=True)


def fold(piece, axis, bit):
    route = [(place, place ^ bit) for place in range(lax.axis_size(axis))]
    other = lax.ppermute(piece, axis, route)
    return (piece.astype(jnp.float32) + other.astype(jnp.float32)).astype(jnp.bfloat16)


def finish(updated, grad):
    rows, columns = grad.shape
    count = lax.axis_size("lon")
    pieces = spread(grad.reshape(count, -1, columns), "lon")
    piece = jnp.sum(pieces.astype(jnp.float32), axis=0).astype(jnp.bfloat16)
    piece = fold(piece, "lat", 8)
    updated, piece = lax.optimization_barrier((updated, piece))
    updated = spread(updated, "lon")
    piece = fold(piece, "lat", 1)
    piece = fold(piece, "lat", 2)
    piece = fold(piece, "lat", 4)
    updated, piece = lax.optimization_barrier((updated, piece))
    copies = jnp.broadcast_to(piece[None], (count, *piece.shape))
    total = spread(copies, "lon").reshape(rows, columns).astype(jnp.float32)
    return updated, total


def route(pairs, lat_count, swap):
    return [
        (comp * lat_count + low, (comp ^ swap) * lat_count + high)
        for comp in range(2)
        for low, high in pairs
    ]


def send(block, pairs, swap):
    return lax.ppermute(block, ("comp", "lat"), route(pairs, lax.axis_size("lat"), swap))


def halos(own, ready):
    lat_dev, lat_count = own.shape[0], lax.axis_size("lat")
    up = [(low, low + 1) for low in range(lat_count - 1)]
    down = [(high, low) for low, high in up]
    low_close = send(own[lat_dev - CLOSE :], up, 1)
    high_close = send(own[:CLOSE], down, 1)
    own, ready = lax.optimization_barrier((own, ready))
    inner = [pair for pair in up if pair[1] % RING]
    rings = range(0, lat_count - RING, RING)
    first_up = [(ring + RING - 1, ring) for ring in rings]
    first_down = [(ring + RING, ring + 2 * RING - 1) for ring in rings]
    turn = lambda pairs: [(high, low) for low, high in pairs]
    mixed = lambda pairs, relay: route(pairs, lat_count, 1) + route(relay, lat_count, 0)
    axes = ("comp", "lat")
    far_up = lax.ppermute(own[lat_dev - REACH : lat_dev - CLOSE], axes, mixed(inner, first_up))
    far_down = lax.ppermute(own[CLOSE:REACH], axes, mixed(turn(inner), first_down))
    over_up = send(far_up, [(ring, ring + RING) for ring in rings], 1)
    over_down = send(far_down, [(ring + 2 * RING - 1, ring + RING - 1) for ring in rings], 1)
    place = lax.axis_index("lat") % RING
    low_far = jnp.where(place == 0, over_up, far_up)
    high_far = jnp.where(place == RING - 1, over_down, far_down)
    return low_close, low_far, high_close, high_far, ready


def local(state, source_cell, remap_weight, sea_mask, spectral_weight, cotangent):
    own = state[0]
    lat_dev, lon_dev, channels = own.shape
    lon_count = lax.axis_size("lon")
    nlon = lon_dev * lon_count
    nlat = lat_dev * lax.axis_size("lat")
    flat = lambda block: block.reshape(-1, channels)

    source = lax.ppermute(own, "comp", [(0, 1), (1, 0)])
    *edges, source = halos(own, source)
    cot = cotangent[0]
    cot = spread(cot, "lon").reshape(lon_count, -1, lon_dev, channels)

    lat = lax.axis_index("lat").astype(jnp.int32).reshape(1)
    partial, close, far = near_part(
        lat, source_cell[0], remap_weight[0], sea_mask[0], flat(source), flat(own)
    )
    forced = edge_part(close, far, partial, *[flat(edge) for edge in edges])
    forced = spread(forced.reshape(own.shape), "lon").reshape(cot.shape)
    table = jnp.asarray(low_pass(nlon, M))
    scale = 1.0 / math.sqrt(2 * M * nlat)
    updated, grad = spectral_part(table, forced, cot, spectral_weight[0], scale)
    updated, total = finish(updated.reshape(own.shape), grad)
    return (updated[None], total[None])


def solution(mesh):
    in_specs = (
        P("comp", "lat", "lon", None),
        P("comp", None, "lat", "lon"),
        P("comp", None, "lat", "lon"),
        P("comp", "lat", "lon"),
        P("comp", None, None),
        P("comp", "lat", "lon", None),
    )
    out_specs = (P("comp", "lat", "lon", None), P("comp", None, None))
    return jax.shard_map(local, mesh=mesh, in_specs=in_specs, out_specs=out_specs, check_vma=False)
```

```python
import functools
import math

import jax
import jax.numpy as jnp
import ml_dtypes
import numpy as np
from jax import lax
from jax.experimental import pallas as pl
from jax.experimental.pallas import tpu as pltpu
from jax.sharding import PartitionSpec as P

M = 384
K = 4
REACH = 8
QUAD = 4
SPAN = 512
RING = 4
CLOSE = 5
NLON_BITS = 10
MIB = 1 << 20


def low_pass(nlon, modes):
    phase = (np.arange(nlon)[:, None] * np.arange(modes)[None, :]) % nlon
    angle = phase * (2.0 * math.pi / nlon)
    norm = 1.0 / math.sqrt(nlon)
    table = np.concatenate([np.cos(angle) * norm, -np.sin(angle) * norm], axis=1)
    table = table.astype(np.float32).astype(ml_dtypes.bfloat16).astype(np.float64)
    factor = np.where(np.arange(modes) == 0, 1.0, 2.0)
    factor = np.concatenate([factor, factor])
    return ((table * factor) @ table.T).astype(np.float32).astype(ml_dtypes.bfloat16)


def near_kernel(
    lat_ref, cell_ref, weight_ref, mask_ref, source_ref, own_ref,
    partial_ref, close_ref, far_ref, place_ref, merged_ref, near_ref,
):
    rows, lon_dev = mask_ref.shape
    first = lat_ref[0] * rows
    sea = mask_ref[...].astype(jnp.float32)
    for term in range(K):
        cell = cell_ref[term]
        place_ref[term] = (lax.shift_right_logical(cell, NLON_BITS) - first) * lon_dev + (
            cell & (lon_dev - 1)
        )
    for term in range(K):
        value = weight_ref[term]
        for other in range(term):
            value = value + jnp.where(place_ref[other] == place_ref[term], weight_ref[other], 0.0)
        merged_ref[term] = value * sea
    ids = lax.broadcasted_iota(jnp.int16, (lon_dev, lon_dev), 0)

    def lines(row):
        place = [place_ref[t, row : row + 1, :].astype(jnp.int16) for t in range(K)]
        share = [merged_ref[t, row : row + 1, :].astype(jnp.bfloat16) for t in range(K)]
        return place, share

    def tile(place, share, start):
        cells = ids + jnp.asarray(start * lon_dev, jnp.int32).astype(jnp.int16)
        out = jnp.zeros((lon_dev, lon_dev), jnp.bfloat16)
        for term in range(K):
            out = jnp.where(place[term] == cells, share[term], out)
        return out

    half = rows // 2
    for row in range(rows):
        place, share = lines(row)
        span = slice(row * lon_dev, (row + 1) * lon_dev)
        low, high = band(row // QUAD, rows)

        def build(source, _):
            at = pl.multiple_of(source * lon_dev, lon_dev)
            near_ref[pl.ds(at, lon_dev), span] = tile(place, share, source)
            return 0

        lax.fori_loop(low, high, build, 0)
        close_first = -CLOSE if row < half else rows

        def build_close(source, _):
            at = pl.multiple_of(source * lon_dev, lon_dev)
            close_ref[pl.ds(at, lon_dev), span] = tile(place, share, source + close_first)
            return 0

        lax.fori_loop(0, CLOSE, build_close, 0)
        if row < QUAD or row >= rows - QUAD:
            far_first = -REACH if row < half else rows + CLOSE
            place_at = row if row < half else row - rows + 2 * QUAD
            far_span = slice(place_at * lon_dev, (place_at + 1) * lon_dev)
            for source in range(REACH - CLOSE):
                far_ref[source * lon_dev : (source + 1) * lon_dev, far_span] = tile(
                    place, share, source + far_first
                )
    size = QUAD * lon_dev
    for block in range(rows // QUAD):
        low, high = band(block, rows)
        span = slice(block * size, (block + 1) * size)
        partial_ref[span, :] = own_ref[span, :].astype(jnp.float32) + across(
            near_ref[low * lon_dev : high * lon_dev, span],
            source_ref[low * lon_dev : high * lon_dev, :],
        )


def across(left, right):
    return lax.dot_general(
        left, right, (((0,), (0,)), ((), ())), preferred_element_type=jnp.float32
    )


def band(block, rows):
    return max(0, block * QUAD - REACH), min(rows, block * QUAD + QUAD + REACH)


def near_part(lat, cells, weight, mask, source, own):
    targets, channels = own.shape
    rows, lon_dev = mask.shape
    vmem = pl.BlockSpec(memory_space=pltpu.VMEM)
    return pl.pallas_call(
        near_kernel,
        out_shape=(
            jax.ShapeDtypeStruct((targets, channels), jnp.float32),
            jax.ShapeDtypeStruct((CLOSE * lon_dev, targets), jnp.bfloat16),
            jax.ShapeDtypeStruct(((REACH - CLOSE) * lon_dev, 2 * QUAD * lon_dev), jnp.bfloat16),
        ),
        in_specs=[pl.BlockSpec(memory_space=pltpu.SMEM)] + [vmem] * 5,
        out_specs=(vmem,) * 3,
        scratch_shapes=[
            pltpu.VMEM(cells.shape, jnp.int32),
            pltpu.VMEM(cells.shape, jnp.float32),
            pltpu.VMEM((targets, targets), jnp.bfloat16),
        ],
        compiler_params=pltpu.CompilerParams(vmem_limit_bytes=40 * MIB),
        cost_estimate=pl.CostEstimate(
            flops=2 * targets * targets * channels, bytes_accessed=16 * MIB, transcendentals=0
        ),
    )(lat, cells, weight, mask, source, own)


def edge_kernel(rows, close_ref, far_ref, partial_ref, low_close_ref, low_far_ref, high_close_ref, high_far_ref, forced_ref):
    lon_dev = low_close_ref.shape[0] // CLOSE
    size, steps = QUAD * lon_dev, rows // QUAD
    for block in range(steps):
        below = block < steps // 2
        place = block if below else steps - 1 - block
        skip = max(0, QUAD * place - (REACH - CLOSE)) * lon_dev
        used = slice(skip, None) if below else slice(0, CLOSE * lon_dev - skip)
        span = slice(block * size, (block + 1) * size)
        halo_ref = low_close_ref if below else high_close_ref
        value = partial_ref[span, :] + across(close_ref[used, span], halo_ref[used, :])
        if place == 0:
            distant_ref = low_far_ref if below else high_far_ref
            far_span = slice(0, size) if below else slice(size, 2 * size)
            value = value + across(far_ref[:, far_span], distant_ref[...])
        forced_ref[span, :] = value.astype(forced_ref.dtype)


def edge_part(close, far, partial, low_close, low_far, high_close, high_far, rows):
    targets, channels = partial.shape
    vmem = pl.BlockSpec(memory_space=pltpu.VMEM)
    return pl.pallas_call(
        functools.partial(edge_kernel, rows),
        out_shape=jax.ShapeDtypeStruct((targets, channels), jnp.bfloat16),
        in_specs=[vmem] * 7,
        out_specs=vmem,
        compiler_params=pltpu.CompilerParams(vmem_limit_bytes=24 * MIB),
        cost_estimate=pl.CostEstimate(
            flops=2 * targets * close.shape[0] * channels, bytes_accessed=10 * MIB, transcendentals=0
        ),
    )(close, far, partial, low_close, low_far, high_close, high_far)


def spectral_kernel(scale, filter_ref, x_ref, cot_ref, weight_ref, out_ref, grad_ref):
    lon_count, rows, lon_dev, channels = x_ref.shape
    weight = weight_ref[...]
    total = jnp.zeros((channels, channels), jnp.float32)
    for row in range(rows):
        x = x_ref[:, row].reshape(-1, channels)
        for first in range(0, lon_count, SPAN // lon_dev):
            blocks = slice(first, first + SPAN // lon_dev)
            part = slice(first * lon_dev, first * lon_dev + SPAN)
            smooth = jnp.dot(filter_ref[part, :], x, preferred_element_type=jnp.float32)
            smooth = smooth.astype(jnp.bfloat16)
            synth = jnp.dot(smooth, weight, preferred_element_type=jnp.float32)
            sigma = 0.5 + 0.5 * jnp.tanh(0.5 * synth)
            mine = x_ref[blocks, row].reshape(SPAN, channels).astype(jnp.float32)
            moved = (mine + synth * sigma).astype(out_ref.dtype)
            out_ref[blocks, row] = moved.reshape(-1, lon_dev, channels)
            cot = cot_ref[blocks, row].reshape(SPAN, channels).astype(jnp.float32)
            grad = (cot * sigma * (1.0 + synth * (1.0 - sigma))).astype(jnp.bfloat16)
            total = total + across(smooth, grad)
    grad_ref[...] = (total * scale).astype(grad_ref.dtype)


def spectral_part(table, x, cot, weight, scale):
    lon_count, rows, lon_dev, channels = x.shape
    nlon = lon_count * lon_dev
    vmem = pl.BlockSpec(memory_space=pltpu.VMEM)
    return pl.pallas_call(
        functools.partial(spectral_kernel, scale),
        out_shape=(
            jax.ShapeDtypeStruct(x.shape, jnp.bfloat16),
            jax.ShapeDtypeStruct((channels, channels), jnp.bfloat16),
        ),
        in_specs=[vmem] * 4,
        out_specs=(vmem, vmem),
        compiler_params=pltpu.CompilerParams(vmem_limit_bytes=32 * MIB),
        cost_estimate=pl.CostEstimate(
            flops=2 * rows * nlon * channels * (nlon + 2 * channels),
            bytes_accessed=8 * MIB,
            transcendentals=rows * nlon * channels,
        ),
    )(table, x, cot, weight)


def spread(block, axis):
    return lax.all_to_all(block, axis, split_axis=0, concat_axis=0, tiled=True)


def fold(piece, step, shift):
    pairs = []
    for place in range(lax.axis_size("lat")):
        at = place // step % RING
        to = (((at + shift) ^ 1) - shift) % RING
        pairs.append((place, place + (to - at) * step))
    other = lax.ppermute(piece, "lat", pairs)
    return (piece.astype(jnp.float32) + other.astype(jnp.float32)).astype(jnp.bfloat16)


def finish(updated, grad):
    rows, columns = grad.shape
    count = lax.axis_size("lon")
    pieces = spread(grad.reshape(count, -1, columns), "lon")
    updated, pieces = lax.optimization_barrier((updated, pieces))
    updated = spread(updated, "lon")
    piece = jnp.sum(pieces.astype(jnp.float32), axis=0).astype(jnp.bfloat16)
    piece = fold(fold(piece, 1, 0), 1, 1)
    piece = fold(fold(piece, RING, 0), RING, 1)
    updated, piece = lax.optimization_barrier((updated, piece))
    copies = jnp.broadcast_to(piece[None], (count, *piece.shape))
    total = spread(copies, "lon").reshape(rows, columns).astype(jnp.float32)
    updated = jnp.where(lax.axis_index("lat") < lax.axis_size("lat"), updated, 0)
    return updated, total


def route(pairs, lat_count, swap):
    return [
        (comp * lat_count + low, (comp ^ swap) * lat_count + high)
        for comp in range(2)
        for low, high in pairs
    ]


def send(block, pairs, swap):
    return lax.ppermute(block, ("comp", "lat"), route(pairs, lax.axis_size("lat"), swap))


def halos(own, ready):
    lat_dev, lat_count = own.shape[0], lax.axis_size("lat")
    up = [(low, low + 1) for low in range(lat_count - 1)]
    down = [(high, low) for low, high in up]
    low_close = send(own[lat_dev - CLOSE :], up, 1)
    high_close = send(own[:CLOSE], down, 1)
    own, ready = lax.optimization_barrier((own, ready))
    inner = [pair for pair in up if pair[1] % RING]
    rings = range(0, lat_count - RING, RING)
    first_up = [(ring + RING - 1, ring) for ring in rings]
    first_down = [(ring + RING, ring + 2 * RING - 1) for ring in rings]
    turn = lambda pairs: [(high, low) for low, high in pairs]
    mixed = lambda pairs, relay: route(pairs, lat_count, 1) + route(relay, lat_count, 0)
    axes = ("comp", "lat")
    far_up = lax.ppermute(own[lat_dev - REACH : lat_dev - CLOSE], axes, mixed(inner, first_up))
    far_down = lax.ppermute(own[CLOSE:REACH], axes, mixed(turn(inner), first_down))
    over_up = send(far_up, [(ring, ring + RING) for ring in rings], 1)
    over_down = send(far_down, [(ring + 2 * RING - 1, ring + RING - 1) for ring in rings], 1)
    place = lax.axis_index("lat") % RING
    low_far = jnp.where(place == 0, over_up, far_up)
    high_far = jnp.where(place == RING - 1, over_down, far_down)
    return low_close, low_far, high_close, high_far, ready


def local(state, source_cell, remap_weight, sea_mask, spectral_weight, cotangent):
    own = state[0]
    lat_dev, lon_dev, channels = own.shape
    lon_count = lax.axis_size("lon")
    nlon = lon_dev * lon_count
    nlat = lat_dev * lax.axis_size("lat")
    flat = lambda block: block.reshape(-1, channels)

    source = lax.ppermute(own, "comp", [(0, 1), (1, 0)])
    *edges, source = halos(own, source)
    cot = cotangent[0]
    cot = spread(cot, "lon").reshape(lon_count, -1, lon_dev, channels)

    lat = lax.axis_index("lat").astype(jnp.int32).reshape(1)
    partial, close, far = near_part(
        lat, source_cell[0], remap_weight[0], sea_mask[0], flat(source), flat(own)
    )
    forced = edge_part(close, far, partial, *[flat(edge) for edge in edges], lat_dev)
    forced = spread(forced.reshape(own.shape), "lon").reshape(cot.shape)
    table = jnp.asarray(low_pass(nlon, M))
    scale = 1.0 / math.sqrt(2 * M * nlat)
    updated, grad = spectral_part(table, forced, cot, spectral_weight[0], scale)
    updated, total = finish(updated.reshape(own.shape), grad)
    return (updated[None], total[None])


def solution(mesh):
    in_specs = (
        P("comp", "lat", "lon", None),
        P("comp", None, "lat", "lon"),
        P("comp", None, "lat", "lon"),
        P("comp", "lat", "lon"),
        P("comp", None, None),
        P("comp", "lat", "lon", None),
    )
    out_specs = (P("comp", "lat", "lon", None), P("comp", None, None))
    return jax.shard_map(local, mesh=mesh, in_specs=in_specs, out_specs=out_specs, check_vma=False)
```

```python
import functools
import math

import jax
import jax.numpy as jnp
import ml_dtypes
import numpy as np
from jax import lax
from jax.experimental import pallas as pl
from jax.experimental.pallas import tpu as pltpu
from jax.sharding import PartitionSpec as P

M = 384
K = 4
REACH = 8
QUAD = 4
SPAN = 512
RING = 4
CLOSE = 5
NLON_BITS = 10
MIB = 1 << 20


def low_pass(nlon, modes):
    phase = (np.arange(nlon)[:, None] * np.arange(modes)[None, :]) % nlon
    angle = phase * (2.0 * math.pi / nlon)
    norm = 1.0 / math.sqrt(nlon)
    table = np.concatenate([np.cos(angle) * norm, -np.sin(angle) * norm], axis=1)
    table = table.astype(np.float32).astype(ml_dtypes.bfloat16).astype(np.float64)
    factor = np.where(np.arange(modes) == 0, 1.0, 2.0)
    factor = np.concatenate([factor, factor])
    return ((table * factor) @ table.T).astype(np.float32).astype(ml_dtypes.bfloat16)


def near_kernel(
    lat_ref, cell_ref, weight_ref, mask_ref, source_ref, own_ref,
    partial_ref, close_ref, far_ref, place_ref, merged_ref, near_ref,
):
    rows, lon_dev = mask_ref.shape
    first = lat_ref[0] * rows
    sea = mask_ref[...].astype(jnp.float32)
    for term in range(K):
        cell = cell_ref[term]
        place_ref[term] = (lax.shift_right_logical(cell, NLON_BITS) - first) * lon_dev + (
            cell & (lon_dev - 1)
        )
    for term in range(K):
        value = weight_ref[term]
        for other in range(term):
            value = value + jnp.where(place_ref[other] == place_ref[term], weight_ref[other], 0.0)
        merged_ref[term] = value * sea
    ids = lax.broadcasted_iota(jnp.int16, (lon_dev, lon_dev), 0)

    def lines(row):
        place = [place_ref[t, row : row + 1, :].astype(jnp.int16) for t in range(K)]
        share = [merged_ref[t, row : row + 1, :].astype(jnp.bfloat16) for t in range(K)]
        return place, share

    def tile(place, share, start):
        cells = ids + jnp.asarray(start * lon_dev, jnp.int32).astype(jnp.int16)
        out = jnp.zeros((lon_dev, lon_dev), jnp.bfloat16)
        for term in range(K):
            out = jnp.where(place[term] == cells, share[term], out)
        return out

    half = rows // 2
    for row in range(rows):
        place, share = lines(row)
        span = slice(row * lon_dev, (row + 1) * lon_dev)
        low, high = band(row // QUAD, rows)

        def build(source, _):
            at = pl.multiple_of(source * lon_dev, lon_dev)
            near_ref[pl.ds(at, lon_dev), span] = tile(place, share, source)
            return 0

        lax.fori_loop(low, high, build, 0)
        close_first = -CLOSE if row < half else rows

        def build_close(source, _):
            at = pl.multiple_of(source * lon_dev, lon_dev)
            close_ref[pl.ds(at, lon_dev), span] = tile(place, share, source + close_first)
            return 0

        lax.fori_loop(0, CLOSE, build_close, 0)
        if row < QUAD or row >= rows - QUAD:
            far_first = -REACH if row < half else rows + CLOSE
            place_at = row if row < half else row - rows + 2 * QUAD
            far_span = slice(place_at * lon_dev, (place_at + 1) * lon_dev)
            for source in range(REACH - CLOSE):
                far_ref[source * lon_dev : (source + 1) * lon_dev, far_span] = tile(
                    place, share, source + far_first
                )
    size = QUAD * lon_dev
    for block in range(rows // QUAD):
        low, high = band(block, rows)
        span = slice(block * size, (block + 1) * size)
        partial_ref[span, :] = own_ref[span, :].astype(jnp.float32) + across(
            near_ref[low * lon_dev : high * lon_dev, span],
            source_ref[low * lon_dev : high * lon_dev, :],
        )


def across(left, right):
    return lax.dot_general(
        left, right, (((0,), (0,)), ((), ())), preferred_element_type=jnp.float32
    )


def band(block, rows):
    return max(0, block * QUAD - REACH), min(rows, block * QUAD + QUAD + REACH)


def near_part(lat, cells, weight, mask, source, own):
    targets, channels = own.shape
    rows, lon_dev = mask.shape
    vmem = pl.BlockSpec(memory_space=pltpu.VMEM)
    return pl.pallas_call(
        near_kernel,
        out_shape=(
            jax.ShapeDtypeStruct((targets, channels), jnp.float32),
            jax.ShapeDtypeStruct((CLOSE * lon_dev, targets), jnp.bfloat16),
            jax.ShapeDtypeStruct(((REACH - CLOSE) * lon_dev, 2 * QUAD * lon_dev), jnp.bfloat16),
        ),
        in_specs=[pl.BlockSpec(memory_space=pltpu.SMEM)] + [vmem] * 5,
        out_specs=(vmem,) * 3,
        scratch_shapes=[
            pltpu.VMEM(cells.shape, jnp.int32),
            pltpu.VMEM(cells.shape, jnp.float32),
            pltpu.VMEM((targets, targets), jnp.bfloat16),
        ],
        compiler_params=pltpu.CompilerParams(vmem_limit_bytes=40 * MIB),
        cost_estimate=pl.CostEstimate(
            flops=2 * targets * targets * channels, bytes_accessed=16 * MIB, transcendentals=0
        ),
    )(lat, cells, weight, mask, source, own)


def edge_kernel(rows, close_ref, far_ref, partial_ref, low_close_ref, low_far_ref, high_close_ref, high_far_ref, forced_ref):
    lon_dev = low_close_ref.shape[0] // CLOSE
    size, steps = QUAD * lon_dev, rows // QUAD
    for block in range(steps):
        below = block < steps // 2
        place = block if below else steps - 1 - block
        skip = max(0, QUAD * place - (REACH - CLOSE)) * lon_dev
        used = slice(skip, None) if below else slice(0, CLOSE * lon_dev - skip)
        span = slice(block * size, (block + 1) * size)
        halo_ref = low_close_ref if below else high_close_ref
        value = partial_ref[span, :] + across(close_ref[used, span], halo_ref[used, :])
        if place == 0:
            distant_ref = low_far_ref if below else high_far_ref
            far_span = slice(0, size) if below else slice(size, 2 * size)
            value = value + across(far_ref[:, far_span], distant_ref[...])
        forced_ref[span, :] = value.astype(forced_ref.dtype)


def edge_part(close, far, partial, low_close, low_far, high_close, high_far, rows):
    targets, channels = partial.shape
    vmem = pl.BlockSpec(memory_space=pltpu.VMEM)
    return pl.pallas_call(
        functools.partial(edge_kernel, rows),
        out_shape=jax.ShapeDtypeStruct((targets, channels), jnp.bfloat16),
        in_specs=[vmem] * 7,
        out_specs=vmem,
        compiler_params=pltpu.CompilerParams(vmem_limit_bytes=24 * MIB),
        cost_estimate=pl.CostEstimate(
            flops=2 * targets * close.shape[0] * channels, bytes_accessed=10 * MIB, transcendentals=0
        ),
    )(close, far, partial, low_close, low_far, high_close, high_far)


def spectral_kernel(scale, filter_ref, x_ref, cot_ref, weight_ref, out_ref, grad_ref):
    lon_count, rows, lon_dev, channels = x_ref.shape
    weight = weight_ref[...]
    total = jnp.zeros((channels, channels), jnp.float32)
    for row in range(rows):
        x = x_ref[:, row].reshape(-1, channels)
        for first in range(0, lon_count, SPAN // lon_dev):
            blocks = slice(first, first + SPAN // lon_dev)
            part = slice(first * lon_dev, first * lon_dev + SPAN)
            smooth = jnp.dot(filter_ref[part, :], x, preferred_element_type=jnp.float32)
            smooth = smooth.astype(jnp.bfloat16)
            synth = jnp.dot(smooth, weight, preferred_element_type=jnp.float32)
            sigma = 0.5 + 0.5 * jnp.tanh(0.5 * synth)
            mine = x_ref[blocks, row].reshape(SPAN, channels).astype(jnp.float32)
            moved = (mine + synth * sigma).astype(out_ref.dtype)
            out_ref[blocks, row] = moved.reshape(-1, lon_dev, channels)
            cot = cot_ref[blocks, row].reshape(SPAN, channels).astype(jnp.float32)
            grad = (cot * sigma * (1.0 + synth * (1.0 - sigma))).astype(jnp.bfloat16)
            total = total + across(smooth, grad)
    grad_ref[...] = (total * scale).astype(grad_ref.dtype)


def spectral_part(table, x, cot, weight, scale):
    lon_count, rows, lon_dev, channels = x.shape
    nlon = lon_count * lon_dev
    vmem = pl.BlockSpec(memory_space=pltpu.VMEM)
    return pl.pallas_call(
        functools.partial(spectral_kernel, scale),
        out_shape=(
            jax.ShapeDtypeStruct(x.shape, jnp.bfloat16),
            jax.ShapeDtypeStruct((channels, channels), jnp.bfloat16),
        ),
        in_specs=[vmem] * 4,
        out_specs=(vmem, vmem),
        compiler_params=pltpu.CompilerParams(vmem_limit_bytes=32 * MIB),
        cost_estimate=pl.CostEstimate(
            flops=2 * rows * nlon * channels * (nlon + 2 * channels),
            bytes_accessed=8 * MIB,
            transcendentals=rows * nlon * channels,
        ),
    )(table, x, cot, weight)


def spread(block, axis):
    return lax.all_to_all(block, axis, split_axis=0, concat_axis=0, tiled=True)


def fold(piece, step, shift):
    pairs = []
    for place in range(lax.axis_size("lat")):
        at = place // step % RING
        to = (((at + shift) ^ 1) - shift) % RING
        pairs.append((place, place + (to - at) * step))
    other = lax.ppermute(piece, "lat", pairs)
    return (piece.astype(jnp.float32) + other.astype(jnp.float32)).astype(jnp.bfloat16)


def gather_sum(piece, step):
    parts = [piece.astype(jnp.float32)]
    for shift in range(1, RING):
        pairs = []
        for place in range(lax.axis_size("lat")):
            at = place // step % RING
            pairs.append((place, place + ((at + shift) % RING - at) * step))
        parts.append(lax.ppermute(piece, "lat", pairs).astype(jnp.float32))
    return ((parts[0] + parts[2]) + (parts[1] + parts[3])).astype(jnp.bfloat16)


def finish(updated, grad):
    rows, columns = grad.shape
    count = lax.axis_size("lon")
    pieces = spread(grad.reshape(count, -1, columns), "lon")
    updated, pieces = lax.optimization_barrier((updated, pieces))
    updated = spread(updated, "lon")
    piece = jnp.sum(pieces.astype(jnp.float32), axis=0).astype(jnp.bfloat16)
    piece = gather_sum(piece, 1)
    piece = gather_sum(piece, RING)
    updated, piece = lax.optimization_barrier((updated, piece))
    copies = jnp.broadcast_to(piece[None], (count, *piece.shape))
    total = spread(copies, "lon").reshape(rows, columns).astype(jnp.float32)
    updated = jnp.where(lax.axis_index("lat") < lax.axis_size("lat"), updated, 0)
    return updated, total


def route(pairs, lat_count, swap):
    return [
        (comp * lat_count + low, (comp ^ swap) * lat_count + high)
        for comp in range(2)
        for low, high in pairs
    ]


def send(block, pairs, swap):
    return lax.ppermute(block, ("comp", "lat"), route(pairs, lax.axis_size("lat"), swap))


def halos(own, ready):
    lat_dev, lat_count = own.shape[0], lax.axis_size("lat")
    up = [(low, low + 1) for low in range(lat_count - 1)]
    down = [(high, low) for low, high in up]
    low_close = send(own[lat_dev - CLOSE :], up, 1)
    high_close = send(own[:CLOSE], down, 1)
    own, ready = lax.optimization_barrier((own, ready))
    inner = [pair for pair in up if pair[1] % RING]
    rings = range(0, lat_count - RING, RING)
    first_up = [(ring + RING - 1, ring) for ring in rings]
    first_down = [(ring + RING, ring + 2 * RING - 1) for ring in rings]
    turn = lambda pairs: [(high, low) for low, high in pairs]
    mixed = lambda pairs, relay: route(pairs, lat_count, 1) + route(relay, lat_count, 0)
    axes = ("comp", "lat")
    far_up = lax.ppermute(own[lat_dev - REACH : lat_dev - CLOSE], axes, mixed(inner, first_up))
    far_down = lax.ppermute(own[CLOSE:REACH], axes, mixed(turn(inner), first_down))
    over_up = send(far_up, [(ring, ring + RING) for ring in rings], 1)
    over_down = send(far_down, [(ring + 2 * RING - 1, ring + RING - 1) for ring in rings], 1)
    place = lax.axis_index("lat") % RING
    low_far = jnp.where(place == 0, over_up, far_up)
    high_far = jnp.where(place == RING - 1, over_down, far_down)
    return low_close, low_far, high_close, high_far, ready


def local(state, source_cell, remap_weight, sea_mask, spectral_weight, cotangent):
    own = state[0]
    lat_dev, lon_dev, channels = own.shape
    lon_count = lax.axis_size("lon")
    nlon = lon_dev * lon_count
    nlat = lat_dev * lax.axis_size("lat")
    flat = lambda block: block.reshape(-1, channels)

    source = lax.ppermute(own, "comp", [(0, 1), (1, 0)])
    *edges, source = halos(own, source)
    cot = cotangent[0]
    cot = spread(cot, "lon").reshape(lon_count, -1, lon_dev, channels)

    lat = lax.axis_index("lat").astype(jnp.int32).reshape(1)
    partial, close, far = near_part(
        lat, source_cell[0], remap_weight[0], sea_mask[0], flat(source), flat(own)
    )
    forced = edge_part(close, far, partial, *[flat(edge) for edge in edges], lat_dev)
    forced = spread(forced.reshape(own.shape), "lon").reshape(cot.shape)
    table = jnp.asarray(low_pass(nlon, M))
    scale = 1.0 / math.sqrt(2 * M * nlat)
    updated, grad = spectral_part(table, forced, cot, spectral_weight[0], scale)
    updated, total = finish(updated.reshape(own.shape), grad)
    return (updated[None], total[None])


def solution(mesh):
    in_specs = (
        P("comp", "lat", "lon", None),
        P("comp", None, "lat", "lon"),
        P("comp", None, "lat", "lon"),
        P("comp", "lat", "lon"),
        P("comp", None, None),
        P("comp", "lat", "lon", None),
    )
    out_specs = (P("comp", "lat", "lon", None), P("comp", None, None))
    return jax.shard_map(local, mesh=mesh, in_specs=in_specs, out_specs=out_specs, check_vma=False)
```

```python
import functools
import math

import jax
import jax.numpy as jnp
import ml_dtypes
import numpy as np
from jax import lax
from jax.experimental import pallas as pl
from jax.experimental.pallas import tpu as pltpu
from jax.sharding import PartitionSpec as P

M = 384
K = 4
REACH = 8
QUAD = 4
SPAN = 512
RING = 4
CLOSE = 5
NLON_BITS = 10
MIB = 1 << 20


def low_pass(nlon, modes):
    phase = (np.arange(nlon)[:, None] * np.arange(modes)[None, :]) % nlon
    angle = phase * (2.0 * math.pi / nlon)
    norm = 1.0 / math.sqrt(nlon)
    table = np.concatenate([np.cos(angle) * norm, -np.sin(angle) * norm], axis=1)
    table = table.astype(np.float32).astype(ml_dtypes.bfloat16).astype(np.float64)
    factor = np.where(np.arange(modes) == 0, 1.0, 2.0)
    factor = np.concatenate([factor, factor])
    return ((table * factor) @ table.T).astype(np.float32).astype(ml_dtypes.bfloat16)


def near_kernel(
    lat_ref, cell_ref, weight_ref, mask_ref, source_ref, own_ref,
    partial_ref, close_ref, far_ref, place_ref, merged_ref, near_ref,
):
    rows, lon_dev = mask_ref.shape
    first = lat_ref[0] * rows
    sea = mask_ref[...].astype(jnp.float32)
    for term in range(K):
        cell = cell_ref[term]
        place_ref[term] = (lax.shift_right_logical(cell, NLON_BITS) - first) * lon_dev + (
            cell & (lon_dev - 1)
        )
    for term in range(K):
        value = weight_ref[term]
        for other in range(term):
            value = value + jnp.where(place_ref[other] == place_ref[term], weight_ref[other], 0.0)
        merged_ref[term] = value * sea
    ids = lax.broadcasted_iota(jnp.int16, (lon_dev, lon_dev), 0)

    def lines(row):
        place = [place_ref[t, row : row + 1, :].astype(jnp.int16) for t in range(K)]
        share = [merged_ref[t, row : row + 1, :].astype(jnp.bfloat16) for t in range(K)]
        return place, share

    def tile(place, share, start):
        cells = ids + jnp.asarray(start * lon_dev, jnp.int32).astype(jnp.int16)
        out = jnp.zeros((lon_dev, lon_dev), jnp.bfloat16)
        for term in range(K):
            out = jnp.where(place[term] == cells, share[term], out)
        return out

    half = rows // 2
    for row in range(rows):
        place, share = lines(row)
        span = slice(row * lon_dev, (row + 1) * lon_dev)
        low, high = band(row // QUAD, rows)

        def build(source, _):
            at = pl.multiple_of(source * lon_dev, lon_dev)
            near_ref[pl.ds(at, lon_dev), span] = tile(place, share, source)
            return 0

        lax.fori_loop(low, high, build, 0)
        close_first = -CLOSE if row < half else rows

        def build_close(source, _):
            at = pl.multiple_of(source * lon_dev, lon_dev)
            close_ref[pl.ds(at, lon_dev), span] = tile(place, share, source + close_first)
            return 0

        lax.fori_loop(0, CLOSE, build_close, 0)
        if row < QUAD or row >= rows - QUAD:
            far_first = -REACH if row < half else rows + CLOSE
            place_at = row if row < half else row - rows + 2 * QUAD
            far_span = slice(place_at * lon_dev, (place_at + 1) * lon_dev)
            for source in range(REACH - CLOSE):
                far_ref[source * lon_dev : (source + 1) * lon_dev, far_span] = tile(
                    place, share, source + far_first
                )
    size = QUAD * lon_dev
    for block in range(rows // QUAD):
        low, high = band(block, rows)
        span = slice(block * size, (block + 1) * size)
        partial_ref[span, :] = own_ref[span, :].astype(jnp.float32) + across(
            near_ref[low * lon_dev : high * lon_dev, span],
            source_ref[low * lon_dev : high * lon_dev, :],
        )


def across(left, right):
    return lax.dot_general(
        left, right, (((0,), (0,)), ((), ())), preferred_element_type=jnp.float32
    )


def band(block, rows):
    return max(0, block * QUAD - REACH), min(rows, block * QUAD + QUAD + REACH)


def near_part(lat, cells, weight, mask, source, own):
    targets, channels = own.shape
    rows, lon_dev = mask.shape
    vmem = pl.BlockSpec(memory_space=pltpu.VMEM)
    return pl.pallas_call(
        near_kernel,
        out_shape=(
            jax.ShapeDtypeStruct((targets, channels), jnp.float32),
            jax.ShapeDtypeStruct((CLOSE * lon_dev, targets), jnp.bfloat16),
            jax.ShapeDtypeStruct(((REACH - CLOSE) * lon_dev, 2 * QUAD * lon_dev), jnp.bfloat16),
        ),
        in_specs=[pl.BlockSpec(memory_space=pltpu.SMEM)] + [vmem] * 5,
        out_specs=(vmem,) * 3,
        scratch_shapes=[
            pltpu.VMEM(cells.shape, jnp.int32),
            pltpu.VMEM(cells.shape, jnp.float32),
            pltpu.VMEM((targets, targets), jnp.bfloat16),
        ],
        compiler_params=pltpu.CompilerParams(vmem_limit_bytes=40 * MIB),
        cost_estimate=pl.CostEstimate(
            flops=2 * targets * targets * channels, bytes_accessed=16 * MIB, transcendentals=0
        ),
    )(lat, cells, weight, mask, source, own)


def edge_kernel(rows, close_ref, far_ref, partial_ref, low_close_ref, low_far_ref, high_close_ref, high_far_ref, forced_ref):
    lon_dev = low_close_ref.shape[0] // CLOSE
    size, steps = QUAD * lon_dev, rows // QUAD
    for block in range(steps):
        below = block < steps // 2
        place = block if below else steps - 1 - block
        skip = max(0, QUAD * place - (REACH - CLOSE)) * lon_dev
        used = slice(skip, None) if below else slice(0, CLOSE * lon_dev - skip)
        span = slice(block * size, (block + 1) * size)
        halo_ref = low_close_ref if below else high_close_ref
        value = partial_ref[span, :] + across(close_ref[used, span], halo_ref[used, :])
        if place == 0:
            distant_ref = low_far_ref if below else high_far_ref
            far_span = slice(0, size) if below else slice(size, 2 * size)
            value = value + across(far_ref[:, far_span], distant_ref[...])
        forced_ref[span, :] = value.astype(forced_ref.dtype)


def edge_part(close, far, partial, low_close, low_far, high_close, high_far, rows):
    targets, channels = partial.shape
    vmem = pl.BlockSpec(memory_space=pltpu.VMEM)
    return pl.pallas_call(
        functools.partial(edge_kernel, rows),
        out_shape=jax.ShapeDtypeStruct((targets, channels), jnp.bfloat16),
        in_specs=[vmem] * 7,
        out_specs=vmem,
        compiler_params=pltpu.CompilerParams(vmem_limit_bytes=24 * MIB),
        cost_estimate=pl.CostEstimate(
            flops=2 * targets * close.shape[0] * channels, bytes_accessed=10 * MIB, transcendentals=0
        ),
    )(close, far, partial, low_close, low_far, high_close, high_far)


def spectral_kernel(scale, filter_ref, x_ref, cot_ref, weight_ref, out_ref, grad_ref):
    lon_count, rows, lon_dev, channels = x_ref.shape
    weight = weight_ref[...]
    total = jnp.zeros((channels, channels), jnp.float32)
    for row in range(rows):
        x = x_ref[:, row].reshape(-1, channels)
        for first in range(0, lon_count, SPAN // lon_dev):
            blocks = slice(first, first + SPAN // lon_dev)
            part = slice(first * lon_dev, first * lon_dev + SPAN)
            smooth = jnp.dot(filter_ref[part, :], x, preferred_element_type=jnp.float32)
            smooth = smooth.astype(jnp.bfloat16)
            synth = jnp.dot(smooth, weight, preferred_element_type=jnp.float32)
            sigma = 0.5 + 0.5 * jnp.tanh(0.5 * synth)
            mine = x_ref[blocks, row].reshape(SPAN, channels).astype(jnp.float32)
            moved = (mine + synth * sigma).astype(out_ref.dtype)
            out_ref[blocks, row] = moved.reshape(-1, lon_dev, channels)
            cot = cot_ref[blocks, row].reshape(SPAN, channels).astype(jnp.float32)
            grad = (cot * sigma * (1.0 + synth * (1.0 - sigma))).astype(jnp.bfloat16)
            total = total + across(smooth, grad)
    grad_ref[...] = (total * scale).astype(grad_ref.dtype)


def spectral_part(table, x, cot, weight, scale):
    lon_count, rows, lon_dev, channels = x.shape
    nlon = lon_count * lon_dev
    vmem = pl.BlockSpec(memory_space=pltpu.VMEM)
    return pl.pallas_call(
        functools.partial(spectral_kernel, scale),
        out_shape=(
            jax.ShapeDtypeStruct(x.shape, jnp.bfloat16),
            jax.ShapeDtypeStruct((channels, channels), jnp.bfloat16),
        ),
        in_specs=[vmem] * 4,
        out_specs=(vmem, vmem),
        compiler_params=pltpu.CompilerParams(vmem_limit_bytes=32 * MIB),
        cost_estimate=pl.CostEstimate(
            flops=2 * rows * nlon * channels * (nlon + 2 * channels),
            bytes_accessed=8 * MIB,
            transcendentals=rows * nlon * channels,
        ),
    )(table, x, cot, weight)


def spread(block, axis):
    return lax.all_to_all(block, axis, split_axis=0, concat_axis=0, tiled=True)


def fold(piece, step, shift):
    pairs = []
    for place in range(lax.axis_size("lat")):
        at = place // step % RING
        to = (((at + shift) ^ 1) - shift) % RING
        pairs.append((place, place + (to - at) * step))
    other = lax.ppermute(piece, "lat", pairs)
    return (piece.astype(jnp.float32) + other.astype(jnp.float32)).astype(jnp.bfloat16)


def gather_sum(piece, step):
    parts = [piece.astype(jnp.float32)]
    for shift in range(1, RING):
        pairs = []
        for place in range(lax.axis_size("lat")):
            at = place // step % RING
            pairs.append((place, place + ((at + shift) % RING - at) * step))
        parts.append(lax.ppermute(piece, "lat", pairs).astype(jnp.float32))
    return ((parts[0] + parts[2]) + (parts[1] + parts[3])).astype(jnp.bfloat16)


def finish(updated, grad):
    rows, columns = grad.shape
    count = lax.axis_size("lon")
    pieces = spread(grad.reshape(count, -1, columns), "lon")
    updated, pieces = lax.optimization_barrier((updated, pieces))
    updated = spread(updated, "lon")
    piece = jnp.sum(pieces.astype(jnp.float32), axis=0).astype(jnp.bfloat16)
    piece = gather_sum(piece, 1)
    piece = gather_sum(piece, RING)
    copies = jnp.broadcast_to(piece[None], (count, *piece.shape))
    updated, copies = lax.optimization_barrier((updated, copies))
    total = spread(copies, "lon").reshape(rows, columns).astype(jnp.float32)
    updated = jnp.where(lax.axis_index("lat") < lax.axis_size("lat"), updated, 0)
    return updated, total


def route(pairs, lat_count, swap):
    return [
        (comp * lat_count + low, (comp ^ swap) * lat_count + high)
        for comp in range(2)
        for low, high in pairs
    ]


def send(block, pairs, swap):
    return lax.ppermute(block, ("comp", "lat"), route(pairs, lax.axis_size("lat"), swap))


def halos(own, ready):
    lat_dev, lat_count = own.shape[0], lax.axis_size("lat")
    up = [(low, low + 1) for low in range(lat_count - 1)]
    down = [(high, low) for low, high in up]
    low_close = send(own[lat_dev - CLOSE :], up, 1)
    high_close = send(own[:CLOSE], down, 1)
    rows_up, rows_down, ready = lax.optimization_barrier(
        (own[lat_dev - REACH : lat_dev - CLOSE], own[CLOSE:REACH], ready)
    )
    inner = [pair for pair in up if pair[1] % RING]
    rings = range(0, lat_count - RING, RING)
    first_up = [(ring + RING - 1, ring) for ring in rings]
    first_down = [(ring + RING, ring + 2 * RING - 1) for ring in rings]
    turn = lambda pairs: [(high, low) for low, high in pairs]
    mixed = lambda pairs, relay: route(pairs, lat_count, 1) + route(relay, lat_count, 0)
    axes = ("comp", "lat")
    far_up = lax.ppermute(rows_up, axes, mixed(inner, first_up))
    far_down = lax.ppermute(rows_down, axes, mixed(turn(inner), first_down))
    over_up = send(far_up, [(ring, ring + RING) for ring in rings], 1)
    over_down = send(far_down, [(ring + 2 * RING - 1, ring + RING - 1) for ring in rings], 1)
    place = lax.axis_index("lat") % RING
    low_far = jnp.where(place == 0, over_up, far_up)
    high_far = jnp.where(place == RING - 1, over_down, far_down)
    return low_close, low_far, high_close, high_far, ready


def local(state, source_cell, remap_weight, sea_mask, spectral_weight, cotangent):
    own = state[0]
    lat_dev, lon_dev, channels = own.shape
    lon_count = lax.axis_size("lon")
    nlon = lon_dev * lon_count
    nlat = lat_dev * lax.axis_size("lat")
    flat = lambda block: block.reshape(-1, channels)

    source = lax.ppermute(own, "comp", [(0, 1), (1, 0)])
    *edges, source = halos(own, source)
    cot = cotangent[0]
    cot = spread(cot, "lon").reshape(lon_count, -1, lon_dev, channels)

    lat = lax.axis_index("lat").astype(jnp.int32).reshape(1)
    partial, close, far = near_part(
        lat, source_cell[0], remap_weight[0], sea_mask[0], flat(source), flat(own)
    )
    forced = edge_part(close, far, partial, *[flat(edge) for edge in edges], lat_dev)
    forced = spread(forced.reshape(own.shape), "lon").reshape(cot.shape)
    table = jnp.asarray(low_pass(nlon, M))
    scale = 1.0 / math.sqrt(2 * M * nlat)
    updated, grad = spectral_part(table, forced, cot, spectral_weight[0], scale)
    updated, total = finish(updated.reshape(own.shape), grad)
    return (updated[None], total[None])


def solution(mesh):
    in_specs = (
        P("comp", "lat", "lon", None),
        P("comp", None, "lat", "lon"),
        P("comp", None, "lat", "lon"),
        P("comp", "lat", "lon"),
        P("comp", None, None),
        P("comp", "lat", "lon", None),
    )
    out_specs = (P("comp", "lat", "lon", None), P("comp", None, None))
    return jax.shard_map(local, mesh=mesh, in_specs=in_specs, out_specs=out_specs, check_vma=False)
```

```python
import functools
import math

import jax
import jax.numpy as jnp
import ml_dtypes
import numpy as np
from jax import lax
from jax.experimental import pallas as pl
from jax.experimental.pallas import tpu as pltpu
from jax.sharding import PartitionSpec as P

M = 384
K = 4
REACH = 8
QUAD = 4
SPAN = 512
RING = 4
CLOSE = 4
NLON_BITS = 10
MIB = 1 << 20


def low_pass(nlon, modes):
    phase = (np.arange(nlon)[:, None] * np.arange(modes)[None, :]) % nlon
    angle = phase * (2.0 * math.pi / nlon)
    norm = 1.0 / math.sqrt(nlon)
    table = np.concatenate([np.cos(angle) * norm, -np.sin(angle) * norm], axis=1)
    table = table.astype(np.float32).astype(ml_dtypes.bfloat16).astype(np.float64)
    factor = np.where(np.arange(modes) == 0, 1.0, 2.0)
    factor = np.concatenate([factor, factor])
    return ((table * factor) @ table.T).astype(np.float32).astype(ml_dtypes.bfloat16)


def near_kernel(
    lat_ref, cell_ref, weight_ref, mask_ref, source_ref, own_ref,
    partial_ref, close_ref, far_ref, place_ref, merged_ref, near_ref,
):
    rows, lon_dev = mask_ref.shape
    first = lat_ref[0] * rows
    sea = mask_ref[...].astype(jnp.float32)
    for term in range(K):
        cell = cell_ref[term]
        place_ref[term] = (lax.shift_right_logical(cell, NLON_BITS) - first) * lon_dev + (
            cell & (lon_dev - 1)
        )
    for term in range(K):
        value = weight_ref[term]
        for other in range(term):
            value = value + jnp.where(place_ref[other] == place_ref[term], weight_ref[other], 0.0)
        merged_ref[term] = value * sea
    ids = lax.broadcasted_iota(jnp.int16, (lon_dev, lon_dev), 0)

    def lines(row):
        place = [place_ref[t, row : row + 1, :].astype(jnp.int16) for t in range(K)]
        share = [merged_ref[t, row : row + 1, :].astype(jnp.bfloat16) for t in range(K)]
        return place, share

    def tile(place, share, start):
        cells = ids + jnp.asarray(start * lon_dev, jnp.int32).astype(jnp.int16)
        out = jnp.zeros((lon_dev, lon_dev), jnp.bfloat16)
        for term in range(K):
            out = jnp.where(place[term] == cells, share[term], out)
        return out

    half = rows // 2
    for row in range(rows):
        place, share = lines(row)
        span = slice(row * lon_dev, (row + 1) * lon_dev)
        low, high = band(row // QUAD, rows)

        def build(source, _):
            at = pl.multiple_of(source * lon_dev, lon_dev)
            near_ref[pl.ds(at, lon_dev), span] = tile(place, share, source)
            return 0

        lax.fori_loop(low, high, build, 0)
        close_first = -CLOSE if row < half else rows

        def build_close(source, _):
            at = pl.multiple_of(source * lon_dev, lon_dev)
            close_ref[pl.ds(at, lon_dev), span] = tile(place, share, source + close_first)
            return 0

        lax.fori_loop(0, CLOSE, build_close, 0)
        if row < QUAD or row >= rows - QUAD:
            far_first = -REACH if row < half else rows + CLOSE
            place_at = row if row < half else row - rows + 2 * QUAD
            far_span = slice(place_at * lon_dev, (place_at + 1) * lon_dev)
            for source in range(REACH - CLOSE):
                far_ref[source * lon_dev : (source + 1) * lon_dev, far_span] = tile(
                    place, share, source + far_first
                )
    size = QUAD * lon_dev
    for block in range(rows // QUAD):
        low, high = band(block, rows)
        span = slice(block * size, (block + 1) * size)
        partial_ref[span, :] = own_ref[span, :].astype(jnp.float32) + across(
            near_ref[low * lon_dev : high * lon_dev, span],
            source_ref[low * lon_dev : high * lon_dev, :],
        )


def across(left, right):
    return lax.dot_general(
        left, right, (((0,), (0,)), ((), ())), preferred_element_type=jnp.float32
    )


def band(block, rows):
    return max(0, block * QUAD - REACH), min(rows, block * QUAD + QUAD + REACH)


def near_part(lat, cells, weight, mask, source, own):
    targets, channels = own.shape
    rows, lon_dev = mask.shape
    vmem = pl.BlockSpec(memory_space=pltpu.VMEM)
    return pl.pallas_call(
        near_kernel,
        out_shape=(
            jax.ShapeDtypeStruct((targets, channels), jnp.float32),
            jax.ShapeDtypeStruct((CLOSE * lon_dev, targets), jnp.bfloat16),
            jax.ShapeDtypeStruct(((REACH - CLOSE) * lon_dev, 2 * QUAD * lon_dev), jnp.bfloat16),
        ),
        in_specs=[pl.BlockSpec(memory_space=pltpu.SMEM)] + [vmem] * 5,
        out_specs=(vmem,) * 3,
        scratch_shapes=[
            pltpu.VMEM(cells.shape, jnp.int32),
            pltpu.VMEM(cells.shape, jnp.float32),
            pltpu.VMEM((targets, targets), jnp.bfloat16),
        ],
        compiler_params=pltpu.CompilerParams(vmem_limit_bytes=40 * MIB),
        cost_estimate=pl.CostEstimate(
            flops=2 * targets * targets * channels, bytes_accessed=16 * MIB, transcendentals=0
        ),
    )(lat, cells, weight, mask, source, own)


def close_kernel(rows, close_ref, partial_ref, low_ref, high_ref, out_ref):
    lon_dev = low_ref.shape[0] // CLOSE
    size, steps = QUAD * lon_dev, rows // QUAD
    for block in range(steps):
        below = block < steps // 2
        place = block if below else steps - 1 - block
        skip = max(0, QUAD * place - (REACH - CLOSE)) * lon_dev
        used = slice(skip, None) if below else slice(0, CLOSE * lon_dev - skip)
        span = slice(block * size, (block + 1) * size)
        halo_ref = low_ref if below else high_ref
        out_ref[span, :] = partial_ref[span, :] + across(close_ref[used, span], halo_ref[used, :])


def far_kernel(rows, far_ref, partial_ref, low_ref, high_ref, forced_ref):
    size = far_ref.shape[1] // 2
    last = partial_ref.shape[0] - size
    forced_ref[size:last, :] = partial_ref[size:last, :].astype(forced_ref.dtype)
    low = partial_ref[:size, :] + across(far_ref[:, :size], low_ref[...])
    forced_ref[:size, :] = low.astype(forced_ref.dtype)
    high = partial_ref[last:, :] + across(far_ref[:, size:], high_ref[...])
    forced_ref[last:, :] = high.astype(forced_ref.dtype)


def edge_call(kernel, dtype, cost, hot, partial, low, high, rows):
    vmem = pl.BlockSpec(memory_space=pltpu.VMEM)
    return pl.pallas_call(
        functools.partial(kernel, rows),
        out_shape=jax.ShapeDtypeStruct(partial.shape, dtype),
        in_specs=[vmem] * 4,
        out_specs=vmem,
        compiler_params=pltpu.CompilerParams(vmem_limit_bytes=24 * MIB),
        cost_estimate=pl.CostEstimate(flops=cost, bytes_accessed=1 << 20, transcendentals=0),
    )(hot, partial, low, high)


def edge_part(close, far, partial, low_close, low_far, high_close, high_far, rows):
    partial = edge_call(close_kernel, jnp.float32, 1 << 30, close, partial, low_close, high_close, rows)
    return edge_call(far_kernel, jnp.bfloat16, 1 << 28, far, partial, low_far, high_far, rows)


def spectral_kernel(scale, filter_ref, x_ref, cot_ref, weight_ref, out_ref, grad_ref):
    lon_count, rows, lon_dev, channels = x_ref.shape
    weight = weight_ref[...]
    total = jnp.zeros((channels, channels), jnp.float32)
    for row in range(rows):
        x = x_ref[:, row].reshape(-1, channels)
        for first in range(0, lon_count, SPAN // lon_dev):
            blocks = slice(first, first + SPAN // lon_dev)
            part = slice(first * lon_dev, first * lon_dev + SPAN)
            smooth = jnp.dot(filter_ref[part, :], x, preferred_element_type=jnp.float32)
            smooth = smooth.astype(jnp.bfloat16)
            synth = jnp.dot(smooth, weight, preferred_element_type=jnp.float32)
            sigma = 0.5 + 0.5 * jnp.tanh(0.5 * synth)
            mine = x_ref[blocks, row].reshape(SPAN, channels).astype(jnp.float32)
            moved = (mine + synth * sigma).astype(out_ref.dtype)
            out_ref[blocks, row] = moved.reshape(-1, lon_dev, channels)
            cot = cot_ref[blocks, row].reshape(SPAN, channels).astype(jnp.float32)
            grad = (cot * sigma * (1.0 + synth * (1.0 - sigma))).astype(jnp.bfloat16)
            total = total + across(smooth, grad)
    grad_ref[...] = (total * scale).astype(grad_ref.dtype)


def spectral_part(table, x, cot, weight, scale):
    lon_count, rows, lon_dev, channels = x.shape
    nlon = lon_count * lon_dev
    vmem = pl.BlockSpec(memory_space=pltpu.VMEM)
    return pl.pallas_call(
        functools.partial(spectral_kernel, scale),
        out_shape=(
            jax.ShapeDtypeStruct(x.shape, jnp.bfloat16),
            jax.ShapeDtypeStruct((channels, channels), jnp.bfloat16),
        ),
        in_specs=[vmem] * 4,
        out_specs=(vmem, vmem),
        compiler_params=pltpu.CompilerParams(vmem_limit_bytes=32 * MIB),
        cost_estimate=pl.CostEstimate(
            flops=2 * rows * nlon * channels * (nlon + 2 * channels),
            bytes_accessed=8 * MIB,
            transcendentals=rows * nlon * channels,
        ),
    )(table, x, cot, weight)


def spread(block, axis):
    return lax.all_to_all(block, axis, split_axis=0, concat_axis=0, tiled=True)


def fold(piece, step, shift):
    pairs = []
    for place in range(lax.axis_size("lat")):
        at = place // step % RING
        to = (((at + shift) ^ 1) - shift) % RING
        pairs.append((place, place + (to - at) * step))
    other = lax.ppermute(piece, "lat", pairs)
    return (piece.astype(jnp.float32) + other.astype(jnp.float32)).astype(jnp.bfloat16)


def gather_sum(piece, step):
    parts = [piece.astype(jnp.float32)]
    for shift in range(1, RING):
        pairs = []
        for place in range(lax.axis_size("lat")):
            at = place // step % RING
            pairs.append((place, place + ((at + shift) % RING - at) * step))
        parts.append(lax.ppermute(piece, "lat", pairs).astype(jnp.float32))
    return ((parts[0] + parts[2]) + (parts[1] + parts[3])).astype(jnp.bfloat16)


def finish(updated, grad):
    rows, columns = grad.shape
    count = lax.axis_size("lon")
    pieces = spread(grad.reshape(count, -1, columns), "lon")
    updated, pieces = lax.optimization_barrier((updated, pieces))
    updated = spread(updated, "lon")
    piece = jnp.sum(pieces.astype(jnp.float32), axis=0).astype(jnp.bfloat16)
    piece = gather_sum(piece, 1)
    piece = gather_sum(piece, RING)
    copies = jnp.broadcast_to(piece[None], (count, *piece.shape))
    updated, copies = lax.optimization_barrier((updated, copies))
    total = spread(copies, "lon").reshape(rows, columns).astype(jnp.float32)
    updated = jnp.where(lax.axis_index("lat") < lax.axis_size("lat"), updated, 0)
    return updated, total


def route(pairs, lat_count, swap):
    return [
        (comp * lat_count + low, (comp ^ swap) * lat_count + high)
        for comp in range(2)
        for low, high in pairs
    ]


def send(block, pairs, swap):
    return lax.ppermute(block, ("comp", "lat"), route(pairs, lax.axis_size("lat"), swap))


def halos(own, ready):
    lat_dev, lat_count = own.shape[0], lax.axis_size("lat")
    up = [(low, low + 1) for low in range(lat_count - 1)]
    down = [(high, low) for low, high in up]
    low_close = send(own[lat_dev - CLOSE :], up, 1)
    high_close = send(own[:CLOSE], down, 1)
    rows_up, rows_down, ready = lax.optimization_barrier(
        (own[lat_dev - REACH : lat_dev - CLOSE], own[CLOSE:REACH], ready)
    )
    inner = [pair for pair in up if pair[1] % RING]
    rings = range(0, lat_count - RING, RING)
    first_up = [(ring + RING - 1, ring) for ring in rings]
    first_down = [(ring + RING, ring + 2 * RING - 1) for ring in rings]
    turn = lambda pairs: [(high, low) for low, high in pairs]
    mixed = lambda pairs, relay: route(pairs, lat_count, 1) + route(relay, lat_count, 0)
    axes = ("comp", "lat")
    far_up = lax.ppermute(rows_up, axes, mixed(inner, first_up))
    far_down = lax.ppermute(rows_down, axes, mixed(turn(inner), first_down))
    over_up = send(far_up, [(ring, ring + RING) for ring in rings], 1)
    over_down = send(far_down, [(ring + 2 * RING - 1, ring + RING - 1) for ring in rings], 1)
    place = lax.axis_index("lat") % RING
    low_far = jnp.where(place == 0, over_up, far_up)
    high_far = jnp.where(place == RING - 1, over_down, far_down)
    return low_close, low_far, high_close, high_far, ready


def local(state, source_cell, remap_weight, sea_mask, spectral_weight, cotangent):
    own = state[0]
    lat_dev, lon_dev, channels = own.shape
    lon_count = lax.axis_size("lon")
    nlon = lon_dev * lon_count
    nlat = lat_dev * lax.axis_size("lat")
    flat = lambda block: block.reshape(-1, channels)

    source = lax.ppermute(own, "comp", [(0, 1), (1, 0)])
    *edges, source = halos(own, source)
    cot = cotangent[0]
    cot = spread(cot, "lon").reshape(lon_count, -1, lon_dev, channels)

    lat = lax.axis_index("lat").astype(jnp.int32).reshape(1)
    partial, close, far = near_part(
        lat, source_cell[0], remap_weight[0], sea_mask[0], flat(source), flat(own)
    )
    forced = edge_part(close, far, partial, *[flat(edge) for edge in edges], lat_dev)
    forced = spread(forced.reshape(own.shape), "lon").reshape(cot.shape)
    table = jnp.asarray(low_pass(nlon, M))
    scale = 1.0 / math.sqrt(2 * M * nlat)
    updated, grad = spectral_part(table, forced, cot, spectral_weight[0], scale)
    updated, total = finish(updated.reshape(own.shape), grad)
    return (updated[None], total[None])


def solution(mesh):
    in_specs = (
        P("comp", "lat", "lon", None),
        P("comp", None, "lat", "lon"),
        P("comp", None, "lat", "lon"),
        P("comp", "lat", "lon"),
        P("comp", None, None),
        P("comp", "lat", "lon", None),
    )
    out_specs = (P("comp", "lat", "lon", None), P("comp", None, None))
    return jax.shard_map(local, mesh=mesh, in_specs=in_specs, out_specs=out_specs, check_vma=False)
```
